256 devices in a mesh: replica: 8 (over z_lo, y), fsdp: 32 (over x, z_hi, core).
Axes of the slice: x: 4, y: 4, z: 8 (z_hi: 4, z_lo: 2; z = z_hi * 2 + z_lo), core: 2. Of those that a mesh axis runs over, the one named last changes fastest.
Arguments:
- tokens: bfloat16 [8, 4096, 6144], P('replica', 'fsdp'), may hold values from -6 to 6
- grad_out: bfloat16 [8, 4096, 6144], P('replica', 'fsdp'), may hold values from -6 to 6
- expert_ids: int32 [8, 4096, 2], P('replica', 'fsdp'), may hold values from 0 to 7, as said below
- gate_share: float32 [8, 4096], P('replica', 'fsdp'), may hold values from 0.05 to 0.95
- up_weight: bfloat16 [8, 6144, 8192], P('replica', None, 'fsdp'), may hold values from -0.078125 to 0.078125
- down_weight: bfloat16 [8, 8192, 6144], P('replica', 'fsdp'), may hold values from -0.0625 to 0.0625
- local_keys: float32 [8, 6144, 512], P('replica', 'fsdp'), may hold values from -6 to 6
- outer_keys: float32 [6144, 512], P('fsdp'), may hold values from -6 to 6
- momentum: float32 [6144, 512], P('fsdp', 'replica'), may hold values from -4 to 4
Outputs:
- input_grad: bfloat16 [8, 4096, 6144], P('replica', 'fsdp')
- new_outer: float32 [6144, 512], P('fsdp')
- new_momentum: float32 [6144, 512], P('fsdp', 'replica')
- outer_copy: bfloat16 [6144, 512], P('fsdp')
The draws below stay inside these ranges and needn't reach their ends.
Inputs may be any that keep to these rules, and one draw needn't show every extreme that they name: `expert_ids`: every token names two different experts. In each replica, each device's 128 consecutive tokens hold exactly 16 that name expert 0.
All inputs are finite; a program needn't handle non-finite values.
Results may differ from the reference program's by a relative error of at most 0.0049.
Values may be sent and summed in bfloat16 or wider, within the bound.
No kernel may reach another device: no remote copies, remote signals or barrier semaphores. Data moves between devices by JAX's collectives and lax.ppermute only.
A program may use at most 128 MiB of HBM per device.

```python
import jax
import jax.numpy as jnp
from jax import lax

D = 6144
FF = 8192
KV = 512
EXPERTS = 8
CAP = 16
TOK_DEV = 128
TOKENS = 4096
REPLICAS = 8
N_REPLICA = 8
N_FSDP = 32


def draw_expert_ids(key, part):
    key = jax.random.fold_in(key, 11)
    blocks = REPLICAS * N_FSDP
    keys = jax.random.split(jax.random.fold_in(key, 1), blocks)
    orders = jax.vmap(lambda one: jax.random.permutation(one, TOK_DEV))(keys)
    ranks = jnp.argsort(orders, axis=1)
    routed = (ranks < CAP).reshape(REPLICAS, TOKENS)
    slot = jax.random.randint(jax.random.fold_in(key, 2), (REPLICAS, TOKENS), 0, 2)
    other = jax.random.randint(jax.random.fold_in(key, 3), (REPLICAS, TOKENS), 1, EXPERTS)
    offset = jax.random.randint(jax.random.fold_in(key, 4), (REPLICAS, TOKENS), 1, EXPERTS - 1)
    second = 1 + (other - 1 + offset) % (EXPERTS - 1)
    first_id = jnp.where(routed, jnp.where(slot == 0, 0, other), other)
    second_id = jnp.where(routed, jnp.where(slot == 0, other, 0), second)
    return jnp.stack([first_id, second_id], axis=-1).astype(jnp.int32)


def strengthened(array, rng, source, target, parts, factor):
    def block_of(axis_at):
        return (jnp.arange(array.shape[axis_at]) // (array.shape[axis_at] // parts)).reshape((-1,) + (1,) * (array.ndim - 1 - axis_at))

    one_side = jax.random.permutation(rng, parts)[block_of(target)]
    second = (block_of(target) + parts // 2) % parts
    return jnp.where((block_of(source) == one_side) | (block_of(source) == second), factor * array, array)


def shard_levels(own_key, shape, shards, smallest, high):
    level, own = 1.0, jax.random.fold_in(own_key, 6)
    for axis_at, shards_of in shards:
        heights = jnp.exp(jax.random.uniform(jax.random.fold_in(own, axis_at), (shards_of,), jnp.float32, smallest / len(shards), high / len(shards)))
        level = level * jnp.repeat(heights, shape[axis_at] // shards_of).reshape([-1 if axis == axis_at else 1 for axis in range(len(shape))])
    return level


def bell_draw(stream_key, shape, spread, reach, cuts=(), kind=jnp.bfloat16):
    values = jax.random.normal(stream_key, shape, jnp.float32) * spread
    if len(cuts) > 0:
        values = shard_levels(stream_key, shape, cuts, -0.22, 0.18) * values
    return jnp.clip(values, min=-reach, max=reach).astype(kind)


def noise_with(own_key, shape, deviation, bound, cuts, heavy, dtype=jnp.bfloat16):
    entries = deviation * jax.random.normal(own_key, shape, jnp.float32)
    if cuts:
        entries = entries * shard_levels(own_key, shape, cuts, -0.22, 0.18)
    return jnp.clip(strengthened(entries, jax.random.fold_in(own_key, 3), *heavy), -bound, bound).astype(dtype)


def setup_inputs(seed: int = 0) -> dict:
    streams_of = jax.random.split(jax.random.key(seed), 10)
    return {
        "tokens": bell_draw(streams_of[0], (REPLICAS, TOKENS, D), 1.0, 6.0, ((0, 8), (1, 32))),
        "grad_out": bell_draw(streams_of[1], (REPLICAS, TOKENS, D), 1.0, 6.0, ((0, 8), (1, 32))),
        "expert_ids": draw_expert_ids(jax.random.fold_in(streams_of[9], 71), 0),
        "gate_share": jnp.clip(0.05 + 0.9 * jax.random.uniform(streams_of[3], (REPLICAS, TOKENS), jnp.float32) ** shard_levels(streams_of[3], (REPLICAS, TOKENS), ((0, 8), (1, 32)), -0.2, 0.2), 0.05, 0.95),
        "up_weight": bell_draw(streams_of[4], (REPLICAS, D, FF), D ** -0.5, 0.078125, ((0, 8), (2, 32))),
        "down_weight": bell_draw(streams_of[5], (REPLICAS, FF, D), FF ** -0.5, 0.0625, ((0, 8), (1, 32))),
        "local_keys": noise_with(streams_of[6], (REPLICAS, D, KV), 1.0, 6.0, ((0, 8), (1, 32)), (0, 2, 8, 2.0), jnp.float32),
        "outer_keys": bell_draw(streams_of[7], (D, KV), 1.0, 6.0, ((0, 32),), jnp.float32),
        "momentum": bell_draw(streams_of[8], (D, KV), 0.5, 4.0, ((0, 32), (1, 8)), jnp.float32),
    }


outer_beta = 0.9
outer_rate = 0.7


def one_replica(tokens_r, grads_r, ids_r, share_r, up_r, down_r):
    first = ids_r[:, 0] == 0
    second = ids_r[:, 1] == 0
    coef = jnp.where(first, share_r, jnp.where(second, 1.0 - share_r, 0.0)).astype(jnp.float32)
    picked = jnp.nonzero(first | second, size=N_FSDP * CAP)[0].astype(jnp.int32)
    rows_in = tokens_r[picked]
    rows_grad = grads_r[picked]
    pre = jnp.dot(rows_in, up_r, preferred_element_type=jnp.float32)
    back = lax.dot_general(rows_grad, down_r, (((1,), (1,)), ((), ())), preferred_element_type=jnp.float32)
    sig = jax.nn.sigmoid(pre)
    hidden_grad = (back * sig * (1.0 + pre * (1.0 - sig))).astype(jnp.bfloat16)
    part = lax.dot_general(hidden_grad, up_r, (((1,), (1,)), ((), ())), preferred_element_type=jnp.float32)
    result = (coef[picked][:, None] * part).astype(jnp.bfloat16)
    return jnp.zeros(tokens_r.shape, jnp.bfloat16).at[picked].set(result)


def reference(tokens, grad_out, expert_ids, gate_share, up_weight, down_weight, local_keys, outer_keys, momentum):
    pieces = []
    for replica in range(N_REPLICA):
        pieces.append(one_replica(tokens[replica], grad_out[replica], expert_ids[replica], gate_share[replica], up_weight[replica], down_weight[replica]))
    input_grad = jnp.stack(pieces, axis=0)
    pseudo = jnp.sum(outer_keys[None, :, :] - local_keys, axis=0) / N_REPLICA
    new_momentum = outer_beta * momentum + pseudo
    new_outer = outer_keys - outer_rate * (pseudo + outer_beta * new_momentum)
    return input_grad, new_outer, new_momentum, new_outer.astype(jnp.bfloat16)
```

```python
import functools

import jax
import jax.numpy as jnp
from jax import lax
from jax.experimental import pallas as pl
from jax.experimental.pallas import tpu as pltpu
from jax.sharding import Mesh
from jax.sharding import PartitionSpec as P

CAP = 16
OUTER_BETA = 0.9
OUTER_RATE = 0.7
MIB = 1 << 20
F32, BF16 = jnp.float32, jnp.bfloat16


def hop(value, axis, step):
    size = lax.axis_size(axis)
    return lax.ppermute(value, axis, [(i, (i + step) % size) for i in range(size)])


def nt(left, right):
    return lax.dot_general(left, right, (((1,), (1,)), ((), ())), preferred_element_type=F32)


def chosen(ids):
    first, second = ids[0:1, :] == 0, ids[1:2, :] == 0
    count = ids.shape[1]
    named = jnp.where(first | second, 1.0, 0.0).astype(F32)
    at = lax.broadcasted_iota(jnp.int32, (count, count), 0)
    upto = lax.broadcasted_iota(jnp.int32, (count, count), 1)
    ones = jnp.where(at <= upto, 1.0, 0.0).astype(BF16)
    wide = jnp.broadcast_to(named, (16, count)).astype(BF16)
    rank = jnp.dot(wide, ones, preferred_element_type=F32)
    slot = lax.broadcasted_iota(jnp.int32, (CAP, count), 0).astype(F32) + 1.0
    return jnp.where((rank == slot) & (named > 0.0), 1.0, 0.0).astype(F32), first, second


def pick_kernel(ids_ref, tokens_ref, grads_ref, out_ref):
    onehot = chosen(ids_ref[...])[0].astype(BF16)
    out_ref[:CAP, :] = jnp.dot(onehot, tokens_ref[...], preferred_element_type=F32).astype(BF16)
    out_ref[CAP:, :] = jnp.dot(onehot, grads_ref[...], preferred_element_type=F32).astype(BF16)


def pick(ids, tokens, grads):
    width = tokens.shape[1]
    return pl.pallas_call(
        pick_kernel,
        out_shape=jax.ShapeDtypeStruct((2 * CAP, width), BF16),
        compiler_params=pltpu.CompilerParams(vmem_limit_bytes=24 * MIB),
        cost_estimate=pl.CostEstimate(flops=2 * 2 * 16 * 128 * width, bytes_accessed=4 * 128 * width, transcendentals=0),
        name="pick",
    )(ids, tokens, grads)


CHUNK = 1024


def expert_kernel(
    own_ref, prev_ref, next_ref, far_in_ref, far_grad_ref, up_a, up_b, down_a, down_b,
    cw_ref, ccw_ref, to_next_ref, to_prev_ref, stay_ref,
    up_a_v, up_b_v, down_a_v, down_b_v, sems,
):
    width, hidden = up_a.shape
    chunks = width // CHUNK
    half = width // 2
    copies = []
    for c in range(chunks):
        part = pl.ds(c * CHUNK, CHUNK)
        pair = [
            pltpu.make_async_copy(up_a.at[part, :], up_a_v.at[part, :], sems.at[0, c]),
            pltpu.make_async_copy(up_b.at[part, :], up_b_v.at[part, :], sems.at[1, c]),
            pltpu.make_async_copy(down_a.at[:, part], down_a_v.at[:, part], sems.at[2, c]),
            pltpu.make_async_copy(down_b.at[:, part], down_b_v.at[:, part], sems.at[3, c]),
        ]
        for copy in pair:
            copy.start()
        copies.append(pair)
    rows = 4 * CAP
    pre_a = pre_b = back_a = back_b = jnp.zeros((rows, hidden), F32)
    for c in range(chunks):
        part = slice(c * CHUNK, (c + 1) * CHUNK)
        for copy in copies[c]:
            copy.wait()
        ins = jnp.concatenate(
            [own_ref[:CAP, part], prev_ref[:CAP, part], next_ref[:CAP, part], far_in_ref[:, part]], axis=0
        )
        grads = jnp.concatenate(
            [own_ref[CAP:, part], prev_ref[CAP:, part], next_ref[CAP:, part], far_grad_ref[:, part]], axis=0
        )
        pre_a += jnp.dot(ins, up_a_v[part, :], preferred_element_type=F32)
        pre_b += jnp.dot(ins, up_b_v[part, :], preferred_element_type=F32)
        back_a += nt(grads, down_a_v[:, part])
        back_b += nt(grads, down_b_v[:, part])

    def hidden_grad(pre, back):
        sig = 1.0 / (1.0 + jnp.exp(-pre))
        return (back * sig * (1.0 + pre * (1.0 - sig))).astype(BF16)

    grad_a, grad_b = hidden_grad(pre_a, back_a), hidden_grad(pre_b, back_b)
    for c in range(chunks):
        part = slice(c * CHUNK, (c + 1) * CHUNK)
        sums = nt(grad_a, up_a_v[part, :]) + nt(grad_b, up_b_v[part, :])
        stay, to_prev, to_next, far = (sums[i * CAP : (i + 1) * CAP] for i in range(4))
        stay_ref[:, part] = stay
        if (c + 1) * CHUNK <= half:
            cw_ref[:, part] = far.astype(BF16)
            ccw_ref[:, part] = to_prev.astype(BF16)
            to_next_ref[:, part] = to_next
        else:
            cw_ref[:, part] = to_next.astype(BF16)
            ccw_ref[:, part] = far.astype(BF16)
            to_prev_ref[:, c * CHUNK - half : (c + 1) * CHUNK - half] = to_prev


def expert(own, prev, nxt, far_in, far_grad, weights):
    width, hidden = weights[0].shape
    whole = pl.BlockSpec(memory_space=pltpu.VMEM)
    return pl.pallas_call(
        expert_kernel,
        out_shape=(
            jax.ShapeDtypeStruct((CAP, width), BF16),
            jax.ShapeDtypeStruct((CAP, width), BF16),
            jax.ShapeDtypeStruct((CAP, width // 2), F32),
            jax.ShapeDtypeStruct((CAP, width // 2), F32),
            jax.ShapeDtypeStruct((CAP, width), F32),
        ),
        in_specs=[whole] * 5 + [pl.BlockSpec(memory_space=pl.ANY)] * 4,
        out_specs=(whole,) * 5,
        scratch_shapes=[
            pltpu.VMEM((width, hidden), BF16),
            pltpu.VMEM((width, hidden), BF16),
            pltpu.VMEM((hidden, width), BF16),
            pltpu.VMEM((hidden, width), BF16),
            pltpu.SemaphoreType.DMA((4, width // CHUNK)),
        ],
        compiler_params=pltpu.CompilerParams(vmem_limit_bytes=32 * MIB),
        cost_estimate=pl.CostEstimate(
            flops=2 * 3 * 4 * CAP * width * 2 * hidden, bytes_accessed=16 * width * hidden, transcendentals=0
        ),
        name="expert",
    )(own, prev, nxt, far_in, far_grad, *weights)


def gather_ring(block, axis):
    prev, nxt = hop(block, axis, 1), hop(block, axis, -1)
    far_in, far_grad = hop(prev[:CAP], axis, 1), hop(nxt[CAP:], axis, -1)
    return prev, nxt, far_in, far_grad


def scatter_ring(cw, ccw, to_next, to_prev, axis):
    half = cw.shape[1] // 2
    from_prev, from_next = hop(cw, axis, 1), hop(ccw, axis, -1)
    on_next = (to_next + from_prev[:, :half].astype(F32)).astype(BF16)
    on_prev = (to_prev + from_next[:, half:].astype(F32)).astype(BF16)
    return from_prev, from_next, hop(on_next, axis, 1), hop(on_prev, axis, -1)


def arrived(stay, got):
    half = stay.shape[1] // 2
    from_prev, from_next, low, high = got
    left = stay[:, :half] + from_next[:, :half].astype(F32) + low.astype(F32)
    right = stay[:, half:] + from_prev[:, half:].astype(F32) + high.astype(F32)
    return left, right


def place_kernel(ids_ref, share_ref, stay_ref, *refs):
    got_x, got_z, out_ref = refs[:4], refs[4:8], refs[8]
    half = stay_ref.shape[1] // 2
    onehot, first, second = chosen(ids_ref[...])
    share = share_ref[...]
    coef = jnp.where(first, share, jnp.where(second, 1.0 - share, 0.0))
    scale = jnp.sum(onehot * coef, axis=1, keepdims=True)
    spread = onehot.T.astype(BF16)
    for part, side in ((slice(0, half), 0), (slice(half, 2 * half), 1)):
        total = stay_ref[:, part]
        for got in (got_x, got_z):
            total += got[1 - side][:, part].astype(F32) + got[2 + side][...].astype(F32)
        result = (scale * total).astype(BF16)
        out_ref[:, part] = jnp.dot(spread, result, preferred_element_type=F32).astype(BF16)


def place(ids, share, stay, got_x, got_z):
    width = stay.shape[1]
    return pl.pallas_call(
        place_kernel,
        out_shape=jax.ShapeDtypeStruct((ids.shape[1], width), BF16),
        compiler_params=pltpu.CompilerParams(vmem_limit_bytes=24 * MIB),
        cost_estimate=pl.CostEstimate(flops=2 * 16 * 128 * width, bytes_accessed=2 * 128 * width, transcendentals=0),
        name="place",
    )(ids, share, stay, *got_x, *got_z)


def outer_step(local_keys, outer_keys, momentum):
    ny, nz = lax.axis_size("y"), lax.axis_size("zlo")
    y, z = lax.axis_index("y"), lax.axis_index("zlo")
    rows, columns = outer_keys.shape
    width = columns // (ny * nz)
    outer_t = outer_keys.T
    term = (outer_t - local_keys.T).reshape(nz, ny, width, rows)

    def at(array, index, axis):
        return lax.dynamic_index_in_dim(array, index, axis, keepdims=False)

    kept = at(term, y, 1)
    for step in range(1, ny):
        kept = kept + hop(at(term, (y + step) % ny, 1), "y", step)
    total = at(kept, z, 0) + hop(at(kept, 1 - z, 0), "zlo", 1)
    pseudo = total / (ny * nz)
    new_momentum = OUTER_BETA * momentum.T + pseudo
    share = pseudo + OUTER_BETA * new_momentum
    other = hop(share, "zlo", 1)
    pair = jnp.where(z == 0, jnp.stack([share, other]), jnp.stack([other, share]))
    full = jnp.zeros((nz, ny, width, rows), F32)
    full = lax.dynamic_update_slice_in_dim(full, pair[:, None], y, 1)
    for step in range(1, ny):
        full = lax.dynamic_update_slice_in_dim(full, hop(pair, "y", step)[:, None], (y - step) % ny, 1)
    new_outer = (outer_t - OUTER_RATE * full.reshape(columns, rows)).T
    return new_outer, new_momentum.T


def per_device(
    tokens, grad_out, expert_ids, gate_share, up_weight, down_weight, local_keys, outer_keys, momentum
):
    ids = expert_ids[0].T
    up, down = up_weight[0], down_weight[0]
    weights = (up, hop(up, "core", 1), down, hop(down, "core", 1))
    mine = pick(ids, tokens[0], grad_out[0])
    z_prev, z_next, z_far_in, z_far_grad = gather_ring(mine, "zh")
    z_far = jnp.concatenate([z_far_in, z_far_grad], axis=0)
    stays, arrivals = [], []
    for block in (mine, z_prev, z_next, z_far):
        cw, ccw, to_next, to_prev, stay = expert(block, *gather_ring(block, "x"), weights)
        stays.append(stay)
        arrivals.append(scatter_ring(cw, ccw, to_next, to_prev, "x"))
    prev_l, prev_r = arrived(stays[1], arrivals[1])
    next_l, next_r = arrived(stays[2], arrivals[2])
    far_l, far_r = arrived(stays[3], arrivals[3])
    cw = jnp.concatenate([far_l, next_r], axis=1).astype(BF16)
    ccw = jnp.concatenate([prev_l, far_r], axis=1).astype(BF16)
    got_z = scatter_ring(cw, ccw, next_l, prev_r, "zh")
    input_grad = place(ids, gate_share, stays[0], arrivals[0], got_z)
    new_outer, new_momentum = outer_step(local_keys[0], outer_keys, momentum)
    return input_grad[None], new_outer, new_momentum, new_outer.astype(BF16)


def solution(mesh):
    fine = Mesh(mesh.devices.reshape(2, 4, 4, 4, 2), ("zlo", "y", "x", "zh", "core"))
    replica, fsdp = ("zlo", "y"), ("x", "zh", "core")
    return jax.shard_map(
        per_device,
        mesh=fine,
        in_specs=(
            P(replica, fsdp, None),
            P(replica, fsdp, None),
            P(replica, fsdp, None),
            P(replica, fsdp),
            P(replica, None, fsdp),
            P(replica, fsdp, None),
            P(replica, fsdp, None),
            P(fsdp, None),
            P(fsdp, replica),
        ),
        out_specs=(P(replica, fsdp, None), P(fsdp, None), P(fsdp, replica), P(fsdp, None)),
        check_vma=False,
    )
```

```python
import functools

import jax
import jax.numpy as jnp
from jax import lax
from jax.experimental import pallas as pl
from jax.experimental.pallas import tpu as pltpu
from jax.sharding import Mesh
from jax.sharding import PartitionSpec as P

CAP = 16
OUTER_BETA = 0.9
OUTER_RATE = 0.7
MIB = 1 << 20
F32, BF16 = jnp.float32, jnp.bfloat16


def hop(value, axis, step):
    size = lax.axis_size(axis)
    return lax.ppermute(value, axis, [(i, (i + step) % size) for i in range(size)])


def mirrored(value, axis, step):
    size = lax.axis_size(axis)
    pairs = []
    for i in range(size):
        pairs.append((2 * i, 2 * ((i + step) % size)))
        pairs.append((2 * i + 1, 2 * ((i - step) % size) + 1))
    return lax.ppermute(value, (axis, "core"), pairs)


def after(value, *earlier):
    return lax.optimization_barrier((value, *earlier))[0]


def nt(left, right):
    return lax.dot_general(left, right, (((1,), (1,)), ((), ())), preferred_element_type=F32)


def chosen(ids):
    first, second = ids[0:1, :] == 0, ids[1:2, :] == 0
    count = ids.shape[1]
    named = jnp.where(first | second, 1.0, 0.0).astype(F32)
    at = lax.broadcasted_iota(jnp.int32, (count, count), 0)
    upto = lax.broadcasted_iota(jnp.int32, (count, count), 1)
    ones = jnp.where(at <= upto, 1.0, 0.0).astype(BF16)
    wide = jnp.broadcast_to(named, (16, count)).astype(BF16)
    rank = jnp.dot(wide, ones, preferred_element_type=F32)
    slot = lax.broadcasted_iota(jnp.int32, (CAP, count), 0).astype(F32) + 1.0
    return jnp.where((rank == slot) & (named > 0.0), 1.0, 0.0).astype(F32), first, second


PICK = 1536


def pick_kernel(ids_ref, tokens, grads, out_ref, tokens_v, grads_v, sems):
    copies = []
    for c in range(tokens.shape[1] // PICK):
        part = pl.ds(c * PICK, PICK)
        pair = (
            pltpu.make_async_copy(tokens.at[:, part], tokens_v.at[:, part], sems.at[0, c]),
            pltpu.make_async_copy(grads.at[:, part], grads_v.at[:, part], sems.at[1, c]),
        )
        for copy in pair:
            copy.start()
        copies.append(pair)
    onehot = chosen(ids_ref[...])[0].astype(BF16)
    for c, pair in enumerate(copies):
        part = slice(c * PICK, (c + 1) * PICK)
        for copy in pair:
            copy.wait()
        out_ref[:CAP, part] = jnp.dot(onehot, tokens_v[:, part], preferred_element_type=F32).astype(BF16)
        out_ref[CAP:, part] = jnp.dot(onehot, grads_v[:, part], preferred_element_type=F32).astype(BF16)


def pick(ids, tokens, grads):
    count, width = tokens.shape
    held = pl.BlockSpec(memory_space=pltpu.VMEM)
    anywhere = pl.BlockSpec(memory_space=pl.ANY)
    return pl.pallas_call(
        pick_kernel,
        out_shape=jax.ShapeDtypeStruct((2 * CAP, width), BF16),
        in_specs=[held, anywhere, anywhere],
        out_specs=held,
        scratch_shapes=[
            pltpu.VMEM((count, width), BF16),
            pltpu.VMEM((count, width), BF16),
            pltpu.SemaphoreType.DMA((2, width // PICK)),
        ],
        compiler_params=pltpu.CompilerParams(vmem_limit_bytes=60 * MIB),
        cost_estimate=pl.CostEstimate(flops=2 * 2 * 16 * 128 * width, bytes_accessed=4 * 128 * width, transcendentals=0),
        name="pick",
    )(ids, tokens, grads)


CHUNK = 1024
WIDE = 2 * CHUNK


def expert_kernel(rings, *refs):
    places = sum(len(ring) for ring in rings)
    count, made = 4 * places, 4 * len(rings)
    blocks, (up_a, up_b, down_a, down_b), outs = refs[:count], refs[count : count + 4], refs[count + 4 : count + 4 + made]
    rows_v, up_a_v, up_b_v, down_a_v, down_b_v, *held, row_sems, sems, out_sems = refs[count + 4 + made :]
    width, hidden = up_a.shape
    rows_in, copies = [], []
    for c in range(width // CHUNK):
        if c % 2 == 0:
            wide = pl.ds(c * CHUNK, WIDE)
            rows_in.append(
                [
                    pltpu.make_async_copy(block.at[:, wide], rows_v.at[i, :, wide], row_sems.at[i, c // 2])
                    for i, block in enumerate(blocks)
                ]
            )
            for copy in rows_in[-1]:
                copy.start()
        part = pl.ds(c * CHUNK, CHUNK)
        group = (
            pltpu.make_async_copy(up_a.at[part, :], up_a_v.at[part, :], sems.at[0, c]),
            pltpu.make_async_copy(up_b.at[part, :], up_b_v.at[part, :], sems.at[1, c]),
            pltpu.make_async_copy(down_a.at[:, part], down_a_v.at[:, part], sems.at[2, c]),
            pltpu.make_async_copy(down_b.at[:, part], down_b_v.at[:, part], sems.at[3, c]),
        )
        for copy in group:
            copy.start()
        copies.append(group)
    pre_a = pre_b = back_a = back_b = jnp.zeros((count * CAP, hidden), F32)
    for c in range(width // CHUNK):
        part = slice(c * CHUNK, (c + 1) * CHUNK)
        if c % 2 == 0:
            for copy in rows_in[c // 2]:
                copy.wait()
        for copy in copies[c]:
            copy.wait()
        ins = rows_v[:, :CAP, part].reshape(count * CAP, CHUNK)
        grads = rows_v[:, CAP:, part].reshape(count * CAP, CHUNK)
        pre_a += jnp.dot(ins, up_a_v[part, :], preferred_element_type=F32)
        pre_b += jnp.dot(ins, up_b_v[part, :], preferred_element_type=F32)
        back_a += nt(grads, down_a_v[:, part])
        back_b += nt(grads, down_b_v[:, part])

    def hidden_grad(pre, back):
        sig = 1.0 / (1.0 + jnp.exp(-pre))
        return (back * sig * (1.0 + pre * (1.0 - sig))).astype(BF16)

    grad_a, grad_b = hidden_grad(pre_a, back_a), hidden_grad(pre_b, back_b)
    leaving = []
    for c in range(width // CHUNK):
        part = slice(c * CHUNK, (c + 1) * CHUNK)
        sums = nt(grad_a, up_a_v[part, :]) + nt(grad_b, up_b_v[part, :])
        for ring, members in enumerate(rings):
            for x in range(4):
                at = 4 * ring + x
                for slot, z in enumerate(members):
                    rows = slice(slot * CAP, (slot + 1) * CAP)
                    held[at][rows, part] = sums[(4 * z + x) * CAP : (4 * z + x + 1) * CAP].astype(held[at].dtype)
                if c % 2 == 1:
                    wide = pl.ds((c - 1) * CHUNK, WIDE)
                    leaving.append(
                        pltpu.make_async_copy(held[at].at[:, wide], outs[at].at[:, wide], out_sems.at[at, c // 2])
                    )
                    leaving[-1].start()
    for copy in leaving:
        copy.wait()


def expert(blocks, weights, rings):
    width, hidden = weights[0].shape
    rows = len(blocks) * CAP
    anywhere = pl.BlockSpec(memory_space=pl.ANY)
    shapes = [(len(members) * CAP, width) for members in rings for _ in range(4)]
    kinds = [F32, BF16, F32, BF16] * len(rings)
    return pl.pallas_call(
        functools.partial(expert_kernel, rings),
        out_shape=tuple(jax.ShapeDtypeStruct(shape, kind) for shape, kind in zip(shapes, kinds)),
        in_specs=[anywhere] * (len(blocks) + 4),
        out_specs=(anywhere,) * len(shapes),
        scratch_shapes=[
            pltpu.VMEM((len(blocks), 2 * CAP, width), BF16),
            pltpu.VMEM((width, hidden), BF16),
            pltpu.VMEM((width, hidden), BF16),
            pltpu.VMEM((hidden, width), BF16),
            pltpu.VMEM((hidden, width), BF16),
            *(pltpu.VMEM(shape, kind) for shape, kind in zip(shapes, kinds)),
            pltpu.SemaphoreType.DMA((len(blocks), width // WIDE)),
            pltpu.SemaphoreType.DMA((4, width // CHUNK)),
            pltpu.SemaphoreType.DMA((len(shapes), width // WIDE)),
        ],
        compiler_params=pltpu.CompilerParams(vmem_limit_bytes=60 * MIB),
        cost_estimate=pl.CostEstimate(
            flops=2 * 3 * rows * width * 2 * hidden, bytes_accessed=16 * width * hidden, transcendentals=0
        ),
        name="expert",
    )(*blocks, *weights)


class Lane:
    def __init__(self, depth):
        self.depth, self.done, self.waits = depth, [], {}

    def hold(self, at, *earlier):
        self.waits[at] = (*self.waits.get(at, ()), *earlier)

    def send(self, value, move):
        waits = self.waits.pop(len(self.done), ())
        if len(self.done) >= self.depth:
            waits = (self.done[-self.depth], *waits)
        if waits:
            value = after(value, *waits)
        self.done.append(move(value))
        return self.done[-1]

    def ring(self, value, axis, step):
        return self.send(value, lambda v: mirrored(v, axis, step))

    def straight(self, value, axis, step):
        return self.send(value, lambda v: hop(v, axis, step))


def gather_ring(lane, block, axis):
    behind, ahead = lane.ring(block, axis, 1), lane.ring(block, axis, -1)
    return block, behind, ahead, lane.ring(behind, axis, 1)


def scatter_ring(lane, to_prev, to_next, far, axis):
    passing = lane.ring(far, axis, 1)
    from_ahead = lane.ring(to_prev, axis, -1)
    onward = (to_next + passing.astype(F32)).astype(BF16)
    return from_ahead, lane.ring(onward, axis, 1)


def arrived(stay, got):
    return stay + got[0].astype(F32) + got[1].astype(F32)


def place_kernel(ids_ref, share_ref, stay_ref, x_a, x_b, z_a, z_b, out_ref):
    onehot, first, second = chosen(ids_ref[...])
    share = share_ref[...]
    coef = jnp.where(first, share, jnp.where(second, 1.0 - share, 0.0))
    scale = jnp.sum(onehot * coef, axis=1, keepdims=True)
    spread = onehot.T.astype(BF16)
    total = stay_ref[...]
    for ref in (x_a, x_b, z_a, z_b):
        total += ref[...].astype(F32)
    result = (scale * total).astype(BF16)
    out_ref[...] = jnp.dot(spread, result, preferred_element_type=F32).astype(BF16)


def place(ids, share, stay, *got):
    count, width = ids.shape[1], stay.shape[1]
    part = width // 3
    return pl.pallas_call(
        place_kernel,
        grid=(3,),
        out_shape=jax.ShapeDtypeStruct((count, width), BF16),
        in_specs=[pl.BlockSpec(ids.shape, lambda i: (0, 0)), pl.BlockSpec(share.shape, lambda i: (0, 0))]
        + [pl.BlockSpec((CAP, part), lambda i: (0, i))] * (1 + len(got)),
        out_specs=pl.BlockSpec((count, part), lambda i: (0, i)),
        compiler_params=pltpu.CompilerParams(vmem_limit_bytes=24 * MIB),
        cost_estimate=pl.CostEstimate(flops=2 * 16 * 128 * width, bytes_accessed=2 * 128 * width, transcendentals=0),
        name="place",
    )(ids, share, stay, *got)


def swap(value, axis, partner):
    size = lax.axis_size(axis)
    pairs = [(2 * i + core, 2 * partner(core, i) + core) for i in range(size) for core in range(2)]
    return lax.ppermute(value, (axis, "core"), pairs)


def outer_sum(lane, term):
    def near(core, i):
        return i ^ 1 if core == 0 else (i + 1) % 4 if i % 2 else (i - 1) % 4

    term = term + lane.send(term, lambda v: swap(v, "y", near))
    term = term + lane.send(term, lambda v: swap(v, "y", lambda core, i: near(1 - core, i)))
    return term + lane.send(term, lambda v: swap(v, "zlo", lambda core, i: 1 - i))


def per_device(
    tokens, grad_out, expert_ids, gate_share, up_weight, down_weight, local_keys, outer_keys, momentum
):
    ids = expert_ids[0].T
    up, down = up_weight[0], down_weight[0]
    over_x, over_z, rest = Lane(2), Lane(1), Lane(1)
    up_other, down_other = hop(up, "core", 1), hop(down, "core", 1)
    mine = pick(ids, tokens[0], grad_out[0])
    own_x = gather_ring(over_x, mine, "x")
    _, behind, ahead, far = gather_ring(over_z, mine, "zh")

    columns, width = outer_keys.shape[1], momentum.shape[1]
    replicas = columns // width
    place_at = lax.axis_index("zlo") * lax.axis_size("y") + lax.axis_index("y")
    held = (lax.broadcasted_iota(jnp.int32, (1, columns), 1) // width) == place_at
    lead = 1.0 + OUTER_BETA
    term = jnp.where(held, OUTER_BETA**2 * jnp.tile(momentum, (1, replicas)), 0.0) - (lead / replicas) * local_keys[0]
    step = lead * outer_keys + outer_sum(rest, after(term, own_x[1]))
    new_outer = outer_keys - OUTER_RATE * step
    share = lax.dynamic_slice_in_dim(step, place_at * width, width, 1)
    new_momentum = OUTER_BETA * momentum + (share - OUTER_BETA**2 * momentum) / lead

    over_x.hold(3, up_other)
    over_x.hold(4, down_other)
    over_x.hold(7, rest.done[0])
    over_x.hold(9, rest.done[1])
    behind_x = gather_ring(over_x, behind, "x")
    ahead_x = gather_ring(over_x, ahead, "x")
    weights = (up, up_other, down, down_other)
    near = expert((*own_x, *behind_x, *ahead_x), weights, ((1, 2), (0,)))
    over_x.hold(11, near[0])
    over_x.hold(12, rest.done[2])
    far_x = gather_ring(over_x, far, "x")
    stay, prev, nxt, far = near[:4]
    pair = arrived(stay, scatter_ring(over_x, prev, nxt, far, "x"))
    over_x.depth = 3
    stay, prev, nxt, far = expert(far_x, weights, ((0,),))
    far = arrived(stay, scatter_ring(over_x, prev, nxt, far, "x"))
    back_z = Lane(2)
    from_ahead = back_z.ring(pair[:CAP].astype(BF16), "zh", -1)
    passing = back_z.ring(far.astype(BF16), "zh", 1)
    from_behind = back_z.ring((pair[CAP:] + passing.astype(F32)).astype(BF16), "zh", 1)
    stay, prev, nxt, far = near[4:]
    got_x = scatter_ring(over_x, prev, nxt, far, "x")
    input_grad = place(ids, gate_share, stay, *got_x, from_ahead, from_behind)
    return input_grad[None], new_outer, new_momentum, new_outer.astype(BF16)


def solution(mesh):
    fine = Mesh(mesh.devices.reshape(2, 4, 4, 4, 2), ("zlo", "y", "x", "zh", "core"))
    replica, fsdp = ("zlo", "y"), ("x", "zh", "core")
    return jax.shard_map(
        per_device,
        mesh=fine,
        in_specs=(
            P(replica, fsdp, None),
            P(replica, fsdp, None),
            P(replica, fsdp, None),
            P(replica, fsdp),
            P(replica, None, fsdp),
            P(replica, fsdp, None),
            P(replica, fsdp, None),
            P(fsdp, None),
            P(fsdp, replica),
        ),
        out_specs=(P(replica, fsdp, None), P(fsdp, None), P(fsdp, replica), P(fsdp, None)),
        check_vma=False,
    )
```

```python
import functools

import jax
import jax.numpy as jnp
from jax import lax
from jax.experimental import pallas as pl
from jax.experimental.pallas import tpu as pltpu
from jax.sharding import Mesh
from jax.sharding import PartitionSpec as P

CAP = 16
OUTER_BETA = 0.9
OUTER_RATE = 0.7
MIB = 1 << 20
F32, BF16 = jnp.float32, jnp.bfloat16


def hop(value, axis, step):
    size = lax.axis_size(axis)
    return lax.ppermute(value, axis, [(i, (i + step) % size) for i in range(size)])


def mirrored(value, axis, step):
    size = lax.axis_size(axis)
    pairs = []
    for i in range(size):
        pairs.append((2 * i, 2 * ((i + step) % size)))
        pairs.append((2 * i + 1, 2 * ((i - step) % size) + 1))
    return lax.ppermute(value, (axis, "core"), pairs)


def after(value, *earlier):
    return lax.optimization_barrier((value, *earlier))[0]


def nt(left, right):
    return lax.dot_general(left, right, (((1,), (1,)), ((), ())), preferred_element_type=F32)


def chosen(ids):
    first, second = ids[0:1, :] == 0, ids[1:2, :] == 0
    count = ids.shape[1]
    named = jnp.where(first | second, 1.0, 0.0).astype(F32)
    at = lax.broadcasted_iota(jnp.int32, (count, count), 0)
    upto = lax.broadcasted_iota(jnp.int32, (count, count), 1)
    ones = jnp.where(at <= upto, 1.0, 0.0).astype(BF16)
    wide = jnp.broadcast_to(named, (16, count)).astype(BF16)
    rank = jnp.dot(wide, ones, preferred_element_type=F32)
    slot = lax.broadcasted_iota(jnp.int32, (CAP, count), 0).astype(F32) + 1.0
    return jnp.where((rank == slot) & (named > 0.0), 1.0, 0.0).astype(F32), first, second


PICK = 1536


def pick_kernel(ids_ref, tokens, grads, out_ref, tokens_v, grads_v, sems):
    copies = []
    for c in range(tokens.shape[1] // PICK):
        part = pl.ds(c * PICK, PICK)
        pair = (
            pltpu.make_async_copy(tokens.at[:, part], tokens_v.at[:, part], sems.at[0, c]),
            pltpu.make_async_copy(grads.at[:, part], grads_v.at[:, part], sems.at[1, c]),
        )
        for copy in pair:
            copy.start()
        copies.append(pair)
    onehot = chosen(ids_ref[...])[0].astype(BF16)
    for c, pair in enumerate(copies):
        part = slice(c * PICK, (c + 1) * PICK)
        for copy in pair:
            copy.wait()
        out_ref[:CAP, part] = jnp.dot(onehot, tokens_v[:, part], preferred_element_type=F32).astype(BF16)
        out_ref[CAP:, part] = jnp.dot(onehot, grads_v[:, part], preferred_element_type=F32).astype(BF16)


def pick(ids, tokens, grads):
    count, width = tokens.shape
    held = pl.BlockSpec(memory_space=pltpu.VMEM)
    anywhere = pl.BlockSpec(memory_space=pl.ANY)
    return pl.pallas_call(
        pick_kernel,
        out_shape=jax.ShapeDtypeStruct((2 * CAP, width), BF16),
        in_specs=[held, anywhere, anywhere],
        out_specs=held,
        scratch_shapes=[
            pltpu.VMEM((count, width), BF16),
            pltpu.VMEM((count, width), BF16),
            pltpu.SemaphoreType.DMA((2, width // PICK)),
        ],
        compiler_params=pltpu.CompilerParams(vmem_limit_bytes=60 * MIB),
        cost_estimate=pl.CostEstimate(flops=2 * 2 * 16 * 128 * width, bytes_accessed=4 * 128 * width, transcendentals=0),
        name="pick",
    )(ids, tokens, grads)


CHUNK = 1024
WIDE = 2 * CHUNK


def expert_kernel(rings, *refs):
    places = sum(len(ring) for ring in rings)
    count, made = 4 * places, 4 * len(rings)
    blocks, (up_a, up_b, down_a, down_b), outs = refs[:count], refs[count : count + 4], refs[count + 4 : count + 4 + made]
    rows_v, up_a_v, up_b_v, down_a_v, down_b_v, *held, row_sems, sems, out_sems = refs[count + 4 + made :]
    width, hidden = up_a.shape
    rows_in, copies = [], []
    for c in range(width // CHUNK):
        if c % 2 == 0:
            wide = pl.ds(c * CHUNK, WIDE)
            rows_in.append(
                [
                    pltpu.make_async_copy(block.at[:, wide], rows_v.at[i, :, wide], row_sems.at[i, c // 2])
                    for i, block in enumerate(blocks)
                ]
            )
            for copy in rows_in[-1]:
                copy.start()
        part = pl.ds(c * CHUNK, CHUNK)
        group = (
            pltpu.make_async_copy(up_a.at[part, :], up_a_v.at[part, :], sems.at[0, c]),
            pltpu.make_async_copy(up_b.at[part, :], up_b_v.at[part, :], sems.at[1, c]),
            pltpu.make_async_copy(down_a.at[:, part], down_a_v.at[:, part], sems.at[2, c]),
            pltpu.make_async_copy(down_b.at[:, part], down_b_v.at[:, part], sems.at[3, c]),
        )
        for copy in group:
            copy.start()
        copies.append(group)
    pre_a = pre_b = back_a = back_b = jnp.zeros((count * CAP, hidden), F32)
    for c in range(width // CHUNK):
        part = slice(c * CHUNK, (c + 1) * CHUNK)
        if c % 2 == 0:
            for copy in rows_in[c // 2]:
                copy.wait()
        for copy in copies[c]:
            copy.wait()
        ins = rows_v[:, :CAP, part].reshape(count * CAP, CHUNK)
        grads = rows_v[:, CAP:, part].reshape(count * CAP, CHUNK)
        pre_a += jnp.dot(ins, up_a_v[part, :], preferred_element_type=F32)
        pre_b += jnp.dot(ins, up_b_v[part, :], preferred_element_type=F32)
        back_a += nt(grads, down_a_v[:, part])
        back_b += nt(grads, down_b_v[:, part])

    def hidden_grad(pre, back):
        sig = 1.0 / (1.0 + jnp.exp(-pre))
        return (back * sig * (1.0 + pre * (1.0 - sig))).astype(BF16)

    grad_a, grad_b = hidden_grad(pre_a, back_a), hidden_grad(pre_b, back_b)
    leaving = []
    for c in range(width // CHUNK):
        part = slice(c * CHUNK, (c + 1) * CHUNK)
        sums = nt(grad_a, up_a_v[part, :]) + nt(grad_b, up_b_v[part, :])
        for ring, members in enumerate(rings):
            for x in range(4):
                at = 4 * ring + x
                for slot, z in enumerate(members):
                    rows = slice(slot * CAP, (slot + 1) * CAP)
                    held[at][rows, part] = sums[(4 * z + x) * CAP : (4 * z + x + 1) * CAP].astype(held[at].dtype)
                if c % 2 == 1:
                    wide = pl.ds((c - 1) * CHUNK, WIDE)
                    leaving.append(
                        pltpu.make_async_copy(held[at].at[:, wide], outs[at].at[:, wide], out_sems.at[at, c // 2])
                    )
                    leaving[-1].start()
    for copy in leaving:
        copy.wait()


def expert(blocks, weights, rings, added):
    width, hidden = weights[0].shape
    rows = len(blocks) * CAP
    anywhere = pl.BlockSpec(memory_space=pl.ANY)
    shapes = [(len(members) * CAP, width) for members in rings for _ in range(4)]
    kinds = [kind for third in added for kind in (F32, BF16, third, BF16)]
    return pl.pallas_call(
        functools.partial(expert_kernel, rings),
        out_shape=tuple(jax.ShapeDtypeStruct(shape, kind) for shape, kind in zip(shapes, kinds)),
        in_specs=[anywhere] * (len(blocks) + 4),
        out_specs=(anywhere,) * len(shapes),
        scratch_shapes=[
            pltpu.VMEM((len(blocks), 2 * CAP, width), BF16),
            pltpu.VMEM((width, hidden), BF16),
            pltpu.VMEM((width, hidden), BF16),
            pltpu.VMEM((hidden, width), BF16),
            pltpu.VMEM((hidden, width), BF16),
            *(pltpu.VMEM(shape, kind) for shape, kind in zip(shapes, kinds)),
            pltpu.SemaphoreType.DMA((len(blocks), width // WIDE)),
            pltpu.SemaphoreType.DMA((4, width // CHUNK)),
            pltpu.SemaphoreType.DMA((len(shapes), width // WIDE)),
        ],
        compiler_params=pltpu.CompilerParams(vmem_limit_bytes=60 * MIB),
        cost_estimate=pl.CostEstimate(
            flops=2 * 3 * rows * width * 2 * hidden, bytes_accessed=16 * width * hidden, transcendentals=0
        ),
        name="expert",
    )(*blocks, *weights)


def after_all(values, *earlier):
    return lax.optimization_barrier((*values, *earlier))[: len(values)]


class Lane:
    def __init__(self, depth):
        self.depth, self.done, self.waits = depth, [], {}

    def hold(self, at, *earlier):
        self.waits[at] = (*self.waits.get(at, ()), *earlier)

    def send(self, value, move):
        waits = self.waits.pop(len(self.done), ())
        if len(self.done) >= self.depth:
            waits = (self.done[-self.depth], *waits)
        if waits:
            value = after(value, *waits)
        self.done.append(move(value))
        return self.done[-1]

    def ring(self, value, axis, step):
        return self.send(value, lambda v: mirrored(v, axis, step))

    def straight(self, value, axis, step):
        return self.send(value, lambda v: hop(v, axis, step))


def gather_ring(lane, block, axis):
    behind, ahead = lane.ring(block, axis, 1), lane.ring(block, axis, -1)
    return block, behind, ahead, lane.ring(behind, axis, 1)


def joined(mine, passing):
    return (mine + passing.astype(F32)).astype(BF16)


def place_kernel(ids_ref, share_ref, stay_ref, *refs):
    *got, out_ref = refs
    onehot, first, second = chosen(ids_ref[...])
    share = share_ref[...]
    coef = jnp.where(first, share, jnp.where(second, 1.0 - share, 0.0))
    scale = jnp.sum(onehot * coef, axis=1, keepdims=True)
    spread = onehot.T.astype(BF16)
    total = stay_ref[...]
    for ref in got:
        total += ref[...].astype(F32)
    result = (scale * total).astype(BF16)
    out_ref[...] = jnp.dot(spread, result, preferred_element_type=F32).astype(BF16)


def place(ids, share, stay, *got):
    count, width = ids.shape[1], stay.shape[1]
    part = width // 3
    return pl.pallas_call(
        place_kernel,
        grid=(3,),
        out_shape=jax.ShapeDtypeStruct((count, width), BF16),
        in_specs=[pl.BlockSpec(ids.shape, lambda i: (0, 0)), pl.BlockSpec(share.shape, lambda i: (0, 0))]
        + [pl.BlockSpec((CAP, part), lambda i: (0, i))] * (1 + len(got)),
        out_specs=pl.BlockSpec((count, part), lambda i: (0, i)),
        compiler_params=pltpu.CompilerParams(vmem_limit_bytes=24 * MIB),
        cost_estimate=pl.CostEstimate(flops=2 * 16 * 128 * width, bytes_accessed=2 * 128 * width, transcendentals=0),
        name="place",
    )(ids, share, stay, *got)


def swap(value, axis, partner):
    size = lax.axis_size(axis)
    pairs = [(2 * i + core, 2 * partner(core, i) + core) for i in range(size) for core in range(2)]
    return lax.ppermute(value, (axis, "core"), pairs)


def outer_sum(lane, term):
    def near(core, i):
        return i ^ 1 if core == 0 else (i + 1) % 4 if i % 2 else (i - 1) % 4

    term = term + lane.send(term, lambda v: swap(v, "y", near))
    term = term + lane.send(term, lambda v: swap(v, "y", lambda core, i: near(1 - core, i)))
    return term + lane.send(term, lambda v: swap(v, "zlo", lambda core, i: 1 - i))


def per_device(
    tokens, grad_out, expert_ids, gate_share, up_weight, down_weight, local_keys, outer_keys, momentum
):
    ids = expert_ids[0].T
    up, down = up_weight[0], down_weight[0]
    over_x, over_z, rest = Lane(2), Lane(1), Lane(1)
    up_other, down_other = hop(up, "core", 1), hop(down, "core", 1)
    mine = pick(ids, tokens[0], grad_out[0])
    own_x = gather_ring(over_x, mine, "x")
    behind = over_z.ring(mine, "zh", 1)
    far = over_z.ring(behind, "zh", 1)
    ahead = over_z.ring(mine, "zh", -1)

    columns, width = outer_keys.shape[1], momentum.shape[1]
    replicas = columns // width
    place_at = lax.axis_index("zlo") * lax.axis_size("y") + lax.axis_index("y")
    held = (lax.broadcasted_iota(jnp.int32, (1, columns), 1) // width) == place_at
    lead = 1.0 + OUTER_BETA
    term = jnp.where(held, OUTER_BETA**2 * jnp.tile(momentum, (1, replicas)), 0.0) - (lead / replicas) * local_keys[0]
    summed = outer_sum(rest, after(term, own_x[1]))
    over_x.hold(3, up_other)
    over_x.hold(4, down_other)
    over_x.hold(7, rest.done[0])
    over_x.hold(9, rest.done[1])
    behind_x = gather_ring(over_x, behind, "x")
    far_x = gather_ring(over_x, far, "x")
    weights = (up, up_other, down, down_other)
    near = expert((*own_x, *behind_x, *far_x), weights, ((1, 2), (0,)), (BF16, F32))
    over_x.hold(11, near[0])
    step = lead * outer_keys + after(summed, near[0])
    new_outer = outer_keys - OUTER_RATE * step
    share = lax.dynamic_slice_in_dim(step, place_at * width, width, 1)
    new_momentum = OUTER_BETA * momentum + (share - OUTER_BETA**2 * momentum) / lead
    ahead_x = gather_ring(over_x, ahead, "x")
    keep_p, prev_p, next_p, far_p = near[:4]
    keep_o, prev_o, next_o, far_o = near[4:]
    keep_a, prev_a, next_a, far_a = expert(ahead_x, weights, ((0,),), (BF16,))

    sent = [hop(far_p, "x", 2), mirrored(prev_p, "x", -1), mirrored(next_p, "x", 1)]
    pair = keep_p + sum(part.astype(F32) for part in after_all(sent, keep_a))
    last_sent = [hop(far_a, "x", 2), mirrored(prev_a, "x", -1), mirrored(next_a, "x", 1)]
    last = keep_a + sum(part.astype(F32) for part in last_sent)
    far_o, prev_o = after_all((far_o, prev_o), far_a)
    own_pass, own_got = mirrored(far_o, "x", 1), mirrored(prev_o, "x", -1)
    own_end = mirrored(joined(next_o, own_pass), "x", 1)
    from_far = hop(pair[CAP:].astype(BF16), "zh", 2)
    from_ahead = mirrored(pair[:CAP].astype(BF16), "zh", -1)
    from_behind = mirrored(last.astype(BF16), "zh", 1)
    input_grad = place(ids, gate_share, keep_o, own_got, own_end, from_ahead, from_behind, from_far)
    return input_grad[None], new_outer, new_momentum, new_outer.astype(BF16)


def solution(mesh):
    fine = Mesh(mesh.devices.reshape(2, 4, 4, 4, 2), ("zlo", "y", "x", "zh", "core"))
    replica, fsdp = ("zlo", "y"), ("x", "zh", "core")
    return jax.shard_map(
        per_device,
        mesh=fine,
        in_specs=(
            P(replica, fsdp, None),
            P(replica, fsdp, None),
            P(replica, fsdp, None),
            P(replica, fsdp),
            P(replica, None, fsdp),
            P(replica, fsdp, None),
            P(replica, fsdp, None),
            P(fsdp, None),
            P(fsdp, replica),
        ),
        out_specs=(P(replica, fsdp, None), P(fsdp, None), P(fsdp, replica), P(fsdp, None)),
        check_vma=False,
    )
```

```python
import functools

import jax
import jax.numpy as jnp
from jax import lax
from jax.experimental import pallas as pl
from jax.experimental.pallas import tpu as pltpu
from jax.sharding import Mesh
from jax.sharding import PartitionSpec as P

CAP = 16
OUTER_BETA = 0.9
OUTER_RATE = 0.7
MIB = 1 << 20
F32, BF16 = jnp.float32, jnp.bfloat16


def hop(value, axis, step):
    size = lax.axis_size(axis)
    return lax.ppermute(value, axis, [(i, (i + step) % size) for i in range(size)])


def mirrored(value, axis, step):
    size = lax.axis_size(axis)
    pairs = []
    for i in range(size):
        pairs.append((2 * i, 2 * ((i + step) % size)))
        pairs.append((2 * i + 1, 2 * ((i - step) % size) + 1))
    return lax.ppermute(value, (axis, "core"), pairs)


def after(value, *earlier):
    return lax.optimization_barrier((value, *earlier))[0]


def nt(left, right):
    return lax.dot_general(left, right, (((1,), (1,)), ((), ())), preferred_element_type=F32)


def chosen(ids):
    first, second = ids[0:1, :] == 0, ids[1:2, :] == 0
    count = ids.shape[1]
    named = jnp.where(first | second, 1.0, 0.0).astype(F32)
    at = lax.broadcasted_iota(jnp.int32, (count, count), 0)
    upto = lax.broadcasted_iota(jnp.int32, (count, count), 1)
    ones = jnp.where(at <= upto, 1.0, 0.0).astype(BF16)
    wide = jnp.broadcast_to(named, (16, count)).astype(BF16)
    rank = jnp.dot(wide, ones, preferred_element_type=F32)
    slot = lax.broadcasted_iota(jnp.int32, (CAP, count), 0).astype(F32) + 1.0
    return jnp.where((rank == slot) & (named > 0.0), 1.0, 0.0).astype(F32), first, second


PICK = 1536


def pick_kernel(ids_ref, tokens, grads, out_ref, tokens_v, grads_v, sems):
    copies = []
    for c in range(tokens.shape[1] // PICK):
        part = pl.ds(c * PICK, PICK)
        pair = (
            pltpu.make_async_copy(tokens.at[:, part], tokens_v.at[:, part], sems.at[0, c]),
            pltpu.make_async_copy(grads.at[:, part], grads_v.at[:, part], sems.at[1, c]),
        )
        for copy in pair:
            copy.start()
        copies.append(pair)
    onehot = chosen(ids_ref[...])[0].astype(BF16)
    for c, pair in enumerate(copies):
        part = slice(c * PICK, (c + 1) * PICK)
        for copy in pair:
            copy.wait()
        out_ref[:CAP, part] = jnp.dot(onehot, tokens_v[:, part], preferred_element_type=F32).astype(BF16)
        out_ref[CAP:, part] = jnp.dot(onehot, grads_v[:, part], preferred_element_type=F32).astype(BF16)


def pick(ids, tokens, grads):
    count, width = tokens.shape
    held = pl.BlockSpec(memory_space=pltpu.VMEM)
    anywhere = pl.BlockSpec(memory_space=pl.ANY)
    return pl.pallas_call(
        pick_kernel,
        out_shape=jax.ShapeDtypeStruct((2 * CAP, width), BF16),
        in_specs=[held, anywhere, anywhere],
        out_specs=held,
        scratch_shapes=[
            pltpu.VMEM((count, width), BF16),
            pltpu.VMEM((count, width), BF16),
            pltpu.SemaphoreType.DMA((2, width // PICK)),
        ],
        compiler_params=pltpu.CompilerParams(vmem_limit_bytes=60 * MIB),
        cost_estimate=pl.CostEstimate(flops=2 * 2 * 16 * 128 * width, bytes_accessed=4 * 128 * width, transcendentals=0),
        name="pick",
    )(ids, tokens, grads)


def expert_kernel(rings, chunk, wide, *refs):
    places = sum(len(ring) for ring in rings)
    count, made = 4 * places, 4 * len(rings)
    blocks, (up_a, up_b, down_a, down_b), outs = refs[:count], refs[count : count + 4], refs[count + 4 : count + 4 + made]
    rows_v, up_a_v, up_b_v, down_a_v, down_b_v, *held, row_sems, sems, out_sems = refs[count + 4 + made :]
    width, hidden = up_a.shape
    per = wide // chunk
    rows_in, copies = [], []
    for c in range(width // chunk):
        if c % per == 0:
            span = pl.ds(c * chunk, wide)
            rows_in.append(
                [
                    pltpu.make_async_copy(block.at[:, span], rows_v.at[i, :, span], row_sems.at[i, c // per])
                    for i, block in enumerate(blocks)
                ]
            )
            for copy in rows_in[-1]:
                copy.start()
        part = pl.ds(c * chunk, chunk)
        group = (
            pltpu.make_async_copy(up_a.at[part, :], up_a_v.at[part, :], sems.at[0, c]),
            pltpu.make_async_copy(up_b.at[part, :], up_b_v.at[part, :], sems.at[1, c]),
            pltpu.make_async_copy(down_a.at[:, part], down_a_v.at[:, part], sems.at[2, c]),
            pltpu.make_async_copy(down_b.at[:, part], down_b_v.at[:, part], sems.at[3, c]),
        )
        for copy in group:
            copy.start()
        copies.append(group)
    pre_a = pre_b = back_a = back_b = jnp.zeros((count * CAP, hidden), F32)
    for c in range(width // chunk):
        part = slice(c * chunk, (c + 1) * chunk)
        if c % per == 0:
            for copy in rows_in[c // per]:
                copy.wait()
        for copy in copies[c]:
            copy.wait()
        ins = rows_v[:, :CAP, part].reshape(count * CAP, chunk)
        grads = rows_v[:, CAP:, part].reshape(count * CAP, chunk)
        pre_a += jnp.dot(ins, up_a_v[part, :], preferred_element_type=F32)
        pre_b += jnp.dot(ins, up_b_v[part, :], preferred_element_type=F32)
        back_a += nt(grads, down_a_v[:, part])
        back_b += nt(grads, down_b_v[:, part])

    def hidden_grad(pre, back):
        sig = 1.0 / (1.0 + jnp.exp(-pre))
        return (back * sig * (1.0 + pre * (1.0 - sig))).astype(BF16)

    grad_a, grad_b = hidden_grad(pre_a, back_a), hidden_grad(pre_b, back_b)
    leaving = []
    for c in range(width // chunk):
        part = slice(c * chunk, (c + 1) * chunk)
        sums = nt(grad_a, up_a_v[part, :]) + nt(grad_b, up_b_v[part, :])
        for ring, members in enumerate(rings):
            for x in range(4):
                at = 4 * ring + x
                for slot, z in enumerate(members):
                    rows = slice(slot * CAP, (slot + 1) * CAP)
                    held[at][rows, part] = sums[(4 * z + x) * CAP : (4 * z + x + 1) * CAP].astype(held[at].dtype)
                if c % per == per - 1:
                    span = pl.ds((c + 1) * chunk - wide, wide)
                    leaving.append(
                        pltpu.make_async_copy(held[at].at[:, span], outs[at].at[:, span], out_sems.at[at, c // per])
                    )
                    leaving[-1].start()
    for copy in leaving:
        copy.wait()


def expert(blocks, weights, rings, added, chunk, wide):
    width, hidden = weights[0].shape
    rows = len(blocks) * CAP
    anywhere = pl.BlockSpec(memory_space=pltpu.HBM)
    shapes = [(len(members) * CAP, width) for members in rings for _ in range(4)]
    kinds = [kind for third in added for kind in (F32, BF16, third, BF16)]
    return pl.pallas_call(
        functools.partial(expert_kernel, rings, chunk, wide),
        out_shape=tuple(jax.ShapeDtypeStruct(shape, kind) for shape, kind in zip(shapes, kinds)),
        in_specs=[anywhere] * (len(blocks) + 4),
        out_specs=(anywhere,) * len(shapes),
        scratch_shapes=[
            pltpu.VMEM((len(blocks), 2 * CAP, width), BF16),
            pltpu.VMEM((width, hidden), BF16),
            pltpu.VMEM((width, hidden), BF16),
            pltpu.VMEM((hidden, width), BF16),
            pltpu.VMEM((hidden, width), BF16),
            *(pltpu.VMEM(shape, kind) for shape, kind in zip(shapes, kinds)),
            pltpu.SemaphoreType.DMA((len(blocks), width // wide)),
            pltpu.SemaphoreType.DMA((4, width // chunk)),
            pltpu.SemaphoreType.DMA((len(shapes), width // wide)),
        ],
        compiler_params=pltpu.CompilerParams(vmem_limit_bytes=60 * MIB),
        cost_estimate=pl.CostEstimate(
            flops=2 * 3 * rows * width * 2 * hidden, bytes_accessed=16 * width * hidden, transcendentals=0
        ),
        name="expert",
    )(*blocks, *weights)


def after_all(values, *earlier):
    return lax.optimization_barrier((*values, *earlier))[: len(values)]


class Lane:
    def __init__(self, depth):
        self.depth, self.done, self.waits = depth, [], {}

    def hold(self, at, *earlier):
        self.waits[at] = (*self.waits.get(at, ()), *earlier)

    def send(self, value, move):
        waits = self.waits.pop(len(self.done), ())
        if len(self.done) >= self.depth:
            waits = (self.done[-self.depth], *waits)
        if waits:
            value = after(value, *waits)
        self.done.append(move(value))
        return self.done[-1]

    def ring(self, value, axis, step):
        return self.send(value, lambda v: mirrored(v, axis, step))

    def straight(self, value, axis, step):
        return self.send(value, lambda v: hop(v, axis, step))


def gather_ring(lane, block, axis):
    behind, ahead = lane.ring(block, axis, 1), lane.ring(block, axis, -1)
    return block, behind, ahead, lane.ring(behind, axis, 1)


def joined(mine, passing):
    return (mine + passing.astype(F32)).astype(BF16)


def place_kernel(ids_ref, share_ref, stay_ref, *refs):
    *got, out_ref = refs
    onehot, first, second = chosen(ids_ref[...])
    share = share_ref[...]
    coef = jnp.where(first, share, jnp.where(second, 1.0 - share, 0.0))
    scale = jnp.sum(onehot * coef, axis=1, keepdims=True)
    spread = onehot.T.astype(BF16)
    total = stay_ref[...]
    for ref in got:
        total += ref[...].astype(F32)
    result = (scale * total).astype(BF16)
    out_ref[...] = jnp.dot(spread, result, preferred_element_type=F32).astype(BF16)


def place(ids, share, stay, *got):
    count, width = ids.shape[1], stay.shape[1]
    part = width // 3
    return pl.pallas_call(
        place_kernel,
        grid=(3,),
        out_shape=jax.ShapeDtypeStruct((count, width), BF16),
        in_specs=[pl.BlockSpec(ids.shape, lambda i: (0, 0)), pl.BlockSpec(share.shape, lambda i: (0, 0))]
        + [pl.BlockSpec((CAP, part), lambda i: (0, i))] * (1 + len(got)),
        out_specs=pl.BlockSpec((count, part), lambda i: (0, i)),
        compiler_params=pltpu.CompilerParams(vmem_limit_bytes=24 * MIB),
        cost_estimate=pl.CostEstimate(flops=2 * 16 * 128 * width, bytes_accessed=2 * 128 * width, transcendentals=0),
        name="place",
    )(ids, share, stay, *got)


def swap(value, axis, partner):
    size = lax.axis_size(axis)
    pairs = [(2 * i + core, 2 * partner(core, i) + core) for i in range(size) for core in range(2)]
    return lax.ppermute(value, (axis, "core"), pairs)


def outer_sum(lane, term):
    def near(core, i):
        return i ^ 1 if core == 0 else (i + 1) % 4 if i % 2 else (i - 1) % 4

    term = term + lane.send(term, lambda v: swap(v, "y", near))
    term = term + lane.send(term, lambda v: swap(v, "y", lambda core, i: near(1 - core, i)))
    return term + lane.send(term, lambda v: swap(v, "zlo", lambda core, i: 1 - i))


def per_device(
    tokens, grad_out, expert_ids, gate_share, up_weight, down_weight, local_keys, outer_keys, momentum
):
    ids = expert_ids[0].T
    up, down = up_weight[0], down_weight[0]
    over_x, over_z, rest = Lane(2), Lane(1), Lane(1)
    up_other, down_other = hop(up, "core", 1), hop(down, "core", 1)
    mine = pick(ids, tokens[0], grad_out[0])
    own_x = gather_ring(over_x, mine, "x")
    behind = over_z.ring(mine, "zh", 1)
    far = over_z.ring(behind, "zh", 1)
    ahead = over_z.ring(mine, "zh", -1)

    columns, width = outer_keys.shape[1], momentum.shape[1]
    replicas = columns // width
    place_at = lax.axis_index("zlo") * lax.axis_size("y") + lax.axis_index("y")
    held = (lax.broadcasted_iota(jnp.int32, (1, columns), 1) // width) == place_at
    lead = 1.0 + OUTER_BETA
    term = jnp.where(held, OUTER_BETA**2 * jnp.tile(momentum, (1, replicas)), 0.0) - (lead / replicas) * local_keys[0]
    summed = outer_sum(rest, after(term, own_x[1]))
    over_x.hold(3, up_other)
    over_x.hold(4, down_other)
    over_x.hold(7, rest.done[0])
    over_x.hold(9, rest.done[1])
    behind_x = gather_ring(over_x, behind, "x")
    far_x = gather_ring(over_x, far, "x")
    weights = (up, up_other, down, down_other)
    near = expert((*own_x, *behind_x, *far_x), weights, ((1, 2), (0,)), (BF16, F32), 1024, 2048)
    step = lead * outer_keys + after(summed, near[0])
    new_outer = outer_keys - OUTER_RATE * step
    share = lax.dynamic_slice_in_dim(step, place_at * width, width, 1)
    new_momentum = OUTER_BETA * momentum + (share - OUTER_BETA**2 * momentum) / lead
    over_x.depth = 3
    ahead_x = (ahead, over_x.ring(ahead, "x", 1), over_x.ring(ahead, "x", -1), over_x.straight(ahead, "x", 2))
    keep_p, prev_p, next_p, far_p = near[:4]
    keep_o, prev_o, next_o, far_o = near[4:]
    keep_a, prev_a, next_a, far_a = expert(ahead_x, weights, ((0,),), (BF16,), 1536, 1536)

    sent = [hop(far_p, "x", 2), mirrored(prev_p, "x", -1), mirrored(next_p, "x", 1)]
    pair = keep_p + sum(part.astype(F32) for part in after_all(sent, keep_a))
    last_sent = [hop(far_a, "x", 2), mirrored(prev_a, "x", -1), mirrored(next_a, "x", 1)]
    last = keep_a + sum(part.astype(F32) for part in last_sent)
    far_o, prev_o = after_all((far_o, prev_o), far_a)
    own_pass, own_got = mirrored(far_o, "x", 1), mirrored(prev_o, "x", -1)
    own_end = mirrored(joined(next_o, own_pass), "x", 1)
    from_far = hop(pair[CAP:].astype(BF16), "zh", 2)
    from_ahead = mirrored(pair[:CAP].astype(BF16), "zh", -1)
    from_behind = mirrored(last.astype(BF16), "zh", 1)
    input_grad = place(ids, gate_share, keep_o, own_got, own_end, from_ahead, from_behind, from_far)
    return input_grad[None], new_outer, new_momentum, new_outer.astype(BF16)


def solution(mesh):
    fine = Mesh(mesh.devices.reshape(2, 4, 4, 4, 2), ("zlo", "y", "x", "zh", "core"))
    replica, fsdp = ("zlo", "y"), ("x", "zh", "core")
    return jax.shard_map(
        per_device,
        mesh=fine,
        in_specs=(
            P(replica, fsdp, None),
            P(replica, fsdp, None),
            P(replica, fsdp, None),
            P(replica, fsdp),
            P(replica, None, fsdp),
            P(replica, fsdp, None),
            P(replica, fsdp, None),
            P(fsdp, None),
            P(fsdp, replica),
        ),
        out_specs=(P(replica, fsdp, None), P(fsdp, None), P(fsdp, replica), P(fsdp, None)),
        check_vma=False,
    )
```

```python
import functools

import jax
import jax.numpy as jnp
from jax import lax
from jax.experimental import pallas as pl
from jax.experimental.pallas import tpu as pltpu
from jax.sharding import Mesh
from jax.sharding import PartitionSpec as P

CAP = 16
OUTER_BETA = 0.9
OUTER_RATE = 0.7
MIB = 1 << 20
F32, BF16 = jnp.float32, jnp.bfloat16


def hop(value, axis, step):
    size = lax.axis_size(axis)
    return lax.ppermute(value, axis, [(i, (i + step) % size) for i in range(size)])


def mirrored(value, axis, step):
    size = lax.axis_size(axis)
    pairs = []
    for i in range(size):
        pairs.append((2 * i, 2 * ((i + step) % size)))
        pairs.append((2 * i + 1, 2 * ((i - step) % size) + 1))
    return lax.ppermute(value, (axis, "core"), pairs)


def after(value, *earlier):
    return lax.optimization_barrier((value, *earlier))[0]


def nt(left, right):
    return lax.dot_general(left, right, (((1,), (1,)), ((), ())), preferred_element_type=F32)


def chosen(ids):
    first, second = ids[0:1, :] == 0, ids[1:2, :] == 0
    count = ids.shape[1]
    named = jnp.where(first | second, 1.0, 0.0).astype(F32)
    at = lax.broadcasted_iota(jnp.int32, (count, count), 0)
    upto = lax.broadcasted_iota(jnp.int32, (count, count), 1)
    ones = jnp.where(at <= upto, 1.0, 0.0).astype(BF16)
    wide = jnp.broadcast_to(named, (16, count)).astype(BF16)
    rank = jnp.dot(wide, ones, preferred_element_type=F32)
    slot = lax.broadcasted_iota(jnp.int32, (CAP, count), 0).astype(F32) + 1.0
    return jnp.where((rank == slot) & (named > 0.0), 1.0, 0.0).astype(F32), first, second


PICK = 1536


def pick_kernel(ids_ref, tokens, grads, out_ref, tokens_v, grads_v, sems):
    copies = []
    for c in range(tokens.shape[1] // PICK):
        part = pl.ds(c * PICK, PICK)
        pair = (
            pltpu.make_async_copy(tokens.at[:, part], tokens_v.at[:, part], sems.at[0, c]),
            pltpu.make_async_copy(grads.at[:, part], grads_v.at[:, part], sems.at[1, c]),
        )
        for copy in pair:
            copy.start()
        copies.append(pair)
    onehot = chosen(ids_ref[...])[0].astype(BF16)
    for c, pair in enumerate(copies):
        part = slice(c * PICK, (c + 1) * PICK)
        for copy in pair:
            copy.wait()
        out_ref[:CAP, part] = jnp.dot(onehot, tokens_v[:, part], preferred_element_type=F32).astype(BF16)
        out_ref[CAP:, part] = jnp.dot(onehot, grads_v[:, part], preferred_element_type=F32).astype(BF16)


def pick(ids, tokens, grads):
    count, width = tokens.shape
    held = pl.BlockSpec(memory_space=pltpu.VMEM)
    anywhere = pl.BlockSpec(memory_space=pl.ANY)
    return pl.pallas_call(
        pick_kernel,
        out_shape=jax.ShapeDtypeStruct((2 * CAP, width), BF16),
        in_specs=[held, anywhere, anywhere],
        out_specs=held,
        scratch_shapes=[
            pltpu.VMEM((count, width), BF16),
            pltpu.VMEM((count, width), BF16),
            pltpu.SemaphoreType.DMA((2, width // PICK)),
        ],
        compiler_params=pltpu.CompilerParams(vmem_limit_bytes=60 * MIB),
        cost_estimate=pl.CostEstimate(flops=2 * 2 * 16 * 128 * width, bytes_accessed=4 * 128 * width, transcendentals=0),
        name="pick",
    )(ids, tokens, grads)


def expert_kernel(rings, chunk, wide, *refs):
    places = sum(len(ring) for ring in rings)
    count, made = 4 * places, 4 * len(rings)
    blocks, (up_a, up_b, down_a, down_b), outs = refs[:count], refs[count : count + 4], refs[count + 4 : count + 4 + made]
    rows_v, up_a_v, up_b_v, down_a_v, down_b_v, *held, row_sems, sems, out_sems = refs[count + 4 + made :]
    width, hidden = up_a.shape
    per = wide // chunk
    rows_in, copies = [], []
    for c in range(width // chunk):
        if c % per == 0:
            span = pl.ds(c * chunk, wide)
            rows_in.append(
                [
                    pltpu.make_async_copy(block.at[:, span], rows_v.at[i, :, span], row_sems.at[i, c // per])
                    for i, block in enumerate(blocks)
                ]
            )
            for copy in rows_in[-1]:
                copy.start()
        part = pl.ds(c * chunk, chunk)
        group = (
            pltpu.make_async_copy(up_a.at[part, :], up_a_v.at[part, :], sems.at[0, c]),
            pltpu.make_async_copy(up_b.at[part, :], up_b_v.at[part, :], sems.at[1, c]),
            pltpu.make_async_copy(down_a.at[:, part], down_a_v.at[:, part], sems.at[2, c]),
            pltpu.make_async_copy(down_b.at[:, part], down_b_v.at[:, part], sems.at[3, c]),
        )
        for copy in group:
            copy.start()
        copies.append(group)
    pre_a = pre_b = back_a = back_b = jnp.zeros((count * CAP, hidden), F32)
    for c in range(width // chunk):
        part = slice(c * chunk, (c + 1) * chunk)
        if c % per == 0:
            for copy in rows_in[c // per]:
                copy.wait()
        for copy in copies[c]:
            copy.wait()
        ins = rows_v[:, :CAP, part].reshape(count * CAP, chunk)
        grads = rows_v[:, CAP:, part].reshape(count * CAP, chunk)
        pre_a += jnp.dot(ins, up_a_v[part, :], preferred_element_type=F32)
        pre_b += jnp.dot(ins, up_b_v[part, :], preferred_element_type=F32)
        back_a += nt(grads, down_a_v[:, part])
        back_b += nt(grads, down_b_v[:, part])

    def hidden_grad(pre, back):
        sig = 1.0 / (1.0 + jnp.exp(-pre))
        return (back * sig * (1.0 + pre * (1.0 - sig))).astype(BF16)

    grad_a, grad_b = hidden_grad(pre_a, back_a), hidden_grad(pre_b, back_b)
    leaving = []
    for c in range(width // chunk):
        part = slice(c * chunk, (c + 1) * chunk)
        sums = nt(grad_a, up_a_v[part, :]) + nt(grad_b, up_b_v[part, :])
        for ring, members in enumerate(rings):
            for x in range(4):
                at = 4 * ring + x
                for slot, z in enumerate(members):
                    rows = slice(slot * CAP, (slot + 1) * CAP)
                    held[at][rows, part] = sums[(4 * z + x) * CAP : (4 * z + x + 1) * CAP].astype(held[at].dtype)
                if c % per == per - 1:
                    span = pl.ds((c + 1) * chunk - wide, wide)
                    leaving.append(
                        pltpu.make_async_copy(held[at].at[:, span], outs[at].at[:, span], out_sems.at[at, c // per])
                    )
                    leaving[-1].start()
    for copy in leaving:
        copy.wait()


def expert(blocks, weights, rings, added, chunk, wide):
    width, hidden = weights[0].shape
    rows = len(blocks) * CAP
    anywhere = pl.BlockSpec(memory_space=pltpu.HBM)
    shapes = [(len(members) * CAP, width) for members in rings for _ in range(4)]
    kinds = [kind for third in added for kind in (F32, BF16, third, BF16)]
    return pl.pallas_call(
        functools.partial(expert_kernel, rings, chunk, wide),
        out_shape=tuple(jax.ShapeDtypeStruct(shape, kind) for shape, kind in zip(shapes, kinds)),
        in_specs=[anywhere] * (len(blocks) + 4),
        out_specs=(anywhere,) * len(shapes),
        scratch_shapes=[
            pltpu.VMEM((len(blocks), 2 * CAP, width), BF16),
            pltpu.VMEM((width, hidden), BF16),
            pltpu.VMEM((width, hidden), BF16),
            pltpu.VMEM((hidden, width), BF16),
            pltpu.VMEM((hidden, width), BF16),
            *(pltpu.VMEM(shape, kind) for shape, kind in zip(shapes, kinds)),
            pltpu.SemaphoreType.DMA((len(blocks), width // wide)),
            pltpu.SemaphoreType.DMA((4, width // chunk)),
            pltpu.SemaphoreType.DMA((len(shapes), width // wide)),
        ],
        compiler_params=pltpu.CompilerParams(vmem_limit_bytes=60 * MIB),
        cost_estimate=pl.CostEstimate(
            flops=2 * 3 * rows * width * 2 * hidden, bytes_accessed=16 * width * hidden, transcendentals=0
        ),
        name="expert",
    )(*blocks, *weights)


def after_all(values, *earlier):
    return lax.optimization_barrier((*values, *earlier))[: len(values)]


class Lane:
    def __init__(self, depth):
        self.depth, self.done, self.waits = depth, [], {}

    def hold(self, at, *earlier):
        self.waits[at] = (*self.waits.get(at, ()), *earlier)

    def send(self, value, move):
        waits = self.waits.pop(len(self.done), ())
        if len(self.done) >= self.depth:
            waits = (self.done[-self.depth], *waits)
        if waits:
            value = after(value, *waits)
        self.done.append(move(value))
        return self.done[-1]

    def ring(self, value, axis, step):
        return self.send(value, lambda v: mirrored(v, axis, step))

    def straight(self, value, axis, step):
        return self.send(value, lambda v: hop(v, axis, step))


def gather_ring(lane, block, axis):
    behind, ahead = lane.ring(block, axis, 1), lane.ring(block, axis, -1)
    return block, behind, ahead, lane.ring(behind, axis, 1)


def place_kernel(ids_ref, share_ref, stay_ref, *refs):
    *got, out_ref = refs
    onehot, first, second = chosen(ids_ref[...])
    share = share_ref[...]
    coef = jnp.where(first, share, jnp.where(second, 1.0 - share, 0.0))
    scale = jnp.sum(onehot * coef, axis=1, keepdims=True)
    spread = onehot.T.astype(BF16)
    total = stay_ref[...]
    for ref in got:
        total += ref[...].astype(F32)
    result = (scale * total).astype(BF16)
    out_ref[...] = jnp.dot(spread, result, preferred_element_type=F32).astype(BF16)


def place(ids, share, stay, *got):
    count, width = ids.shape[1], stay.shape[1]
    part = width // 3
    return pl.pallas_call(
        place_kernel,
        grid=(3,),
        out_shape=jax.ShapeDtypeStruct((count, width), BF16),
        in_specs=[pl.BlockSpec(ids.shape, lambda i: (0, 0)), pl.BlockSpec(share.shape, lambda i: (0, 0))]
        + [pl.BlockSpec((CAP, part), lambda i: (0, i))] * (1 + len(got)),
        out_specs=pl.BlockSpec((count, part), lambda i: (0, i)),
        compiler_params=pltpu.CompilerParams(vmem_limit_bytes=24 * MIB),
        cost_estimate=pl.CostEstimate(flops=2 * 16 * 128 * width, bytes_accessed=2 * 128 * width, transcendentals=0),
        name="place",
    )(ids, share, stay, *got)


def swap(value, axis, partner):
    size = lax.axis_size(axis)
    pairs = [(2 * i + core, 2 * partner(core, i) + core) for i in range(size) for core in range(2)]
    return lax.ppermute(value, (axis, "core"), pairs)


def outer_sum(lane, term):
    def near(core, i):
        return i ^ 1 if core == 0 else (i + 1) % 4 if i % 2 else (i - 1) % 4

    term = term + lane.send(term, lambda v: swap(v, "y", near))
    term = term + lane.send(term, lambda v: swap(v, "y", lambda core, i: near(1 - core, i)))
    return term + lane.send(term, lambda v: swap(v, "zlo", lambda core, i: 1 - i))


def per_device(
    tokens, grad_out, expert_ids, gate_share, up_weight, down_weight, local_keys, outer_keys, momentum
):
    ids = expert_ids[0].T
    up, down = up_weight[0], down_weight[0]
    over_x, over_z, rest = Lane(2), Lane(1), Lane(1)
    up_other, down_other = hop(up, "core", 1), hop(down, "core", 1)
    mine = pick(ids, tokens[0], grad_out[0])
    own_x = gather_ring(over_x, mine, "x")
    behind = over_z.ring(mine, "zh", 1)
    far = over_z.ring(behind, "zh", 1)
    ahead = over_z.ring(mine, "zh", -1)

    columns, width = outer_keys.shape[1], momentum.shape[1]
    replicas = columns // width
    place_at = lax.axis_index("zlo") * lax.axis_size("y") + lax.axis_index("y")
    held = (lax.broadcasted_iota(jnp.int32, (1, columns), 1) // width) == place_at
    lead = 1.0 + OUTER_BETA
    term = jnp.where(held, OUTER_BETA**2 * jnp.tile(momentum, (1, replicas)), 0.0) - (lead / replicas) * local_keys[0]
    summed = outer_sum(rest, after(term, own_x[1]))
    over_x.hold(3, up_other)
    over_x.hold(4, down_other)
    over_x.hold(7, rest.done[0])
    over_x.hold(9, rest.done[1])
    behind_x = gather_ring(over_x, behind, "x")
    far_x = gather_ring(over_x, far, "x")
    weights = (up, up_other, down, down_other)
    near = expert((*own_x, *behind_x, *far_x), weights, ((1, 2), (0,)), (BF16, BF16), 1024, 2048)
    step = lead * outer_keys + after(summed, near[0])
    new_outer = outer_keys - OUTER_RATE * step
    share = lax.dynamic_slice_in_dim(step, place_at * width, width, 1)
    new_momentum = OUTER_BETA * momentum + (share - OUTER_BETA**2 * momentum) / lead
    over_x.depth = 3
    ahead_x = (ahead, over_x.ring(ahead, "x", 1), over_x.ring(ahead, "x", -1), over_x.straight(ahead, "x", 2))
    keep_p, prev_p, next_p, far_p = near[:4]
    keep_o, prev_o, next_o, far_o = near[4:]
    keep_a, prev_a, next_a, far_a = expert(ahead_x, weights, ((0,),), (BF16,), 1536, 1536)

    sent = [hop(far_p, "x", 2), mirrored(prev_p, "x", -1), mirrored(next_p, "x", 1)]
    pair = keep_p + sum(part.astype(F32) for part in after_all(sent, keep_a))
    last_sent = [hop(far_a, "x", 2), mirrored(prev_a, "x", -1), mirrored(next_a, "x", 1)]
    last = keep_a + sum(part.astype(F32) for part in last_sent)
    far_o, prev_o, next_o = after_all((far_o, prev_o, next_o), far_a)
    own_sent = [hop(far_o, "x", 2), mirrored(prev_o, "x", -1), mirrored(next_o, "x", 1)]
    from_far = hop(pair[CAP:].astype(BF16), "zh", 2)
    from_ahead = mirrored(pair[:CAP].astype(BF16), "zh", -1)
    from_behind = mirrored(last.astype(BF16), "zh", 1)
    input_grad = place(ids, gate_share, keep_o, *own_sent, from_ahead, from_behind, from_far)
    return input_grad[None], new_outer, new_momentum, new_outer.astype(BF16)


def solution(mesh):
    fine = Mesh(mesh.devices.reshape(2, 4, 4, 4, 2), ("zlo", "y", "x", "zh", "core"))
    replica, fsdp = ("zlo", "y"), ("x", "zh", "core")
    return jax.shard_map(
        per_device,
        mesh=fine,
        in_specs=(
            P(replica, fsdp, None),
            P(replica, fsdp, None),
            P(replica, fsdp, None),
            P(replica, fsdp),
            P(replica, None, fsdp),
            P(replica, fsdp, None),
            P(replica, fsdp, None),
            P(fsdp, None),
            P(fsdp, replica),
        ),
        out_specs=(P(replica, fsdp, None), P(fsdp, None), P(fsdp, replica), P(fsdp, None)),
        check_vma=False,
    )
```
